1024 devices in a mesh: enc: 8 (over y), dp: 64 (over x, z), rep: 2 (over core).
Axes of the slice: x: 4, y: 8, z: 16, core: 2. Of those that a mesh axis runs over, the one named last changes fastest.
Arguments:
- feat_sig: bfloat16 [32768, 1152], P(('dp', 'rep'), 'enc'), may hold values from -6 to 6
- feat_cnx: bfloat16 [32768, 3072], P(('dp', 'rep'), 'enc'), may hold values from -6 to 6
- cotangent: bfloat16 [32768, 2048], P(('dp', 'rep'), 'enc'), may hold values from -24 to 24
- w_sig: bfloat16 [2048, 1152], P(None, 'enc'), may hold values from -0.09375 to 0.09375
- w_cnx: bfloat16 [2048, 3072], P(None, 'enc'), may hold values from -0.09375 to 0.09375
- lengths: int32 [128, 64], P(('dp', 'rep')), may hold values from 1 to 4, as said below
- enc_of: int32 [128, 64], P(('dp', 'rep')), may hold values from 0 to 63, each once within a row
- owner_of: int32 [128, 64], P(('dp', 'rep')), may hold values from 0 to 63, each once within a row
- pre_sig: bfloat16 [32768, 1152], P(('dp', 'rep'), 'enc'), may hold values from -6 to 6
- pre_cnx: bfloat16 [32768, 3072], P(('dp', 'rep'), 'enc'), may hold values from -6 to 6
- gain_sig: float32 [1152], P('enc'), may hold values from 0.5 to 2
- gain_cnx: float32 [3072], P('enc'), may hold values from 0.5 to 2
Outputs:
- grad_w_sig: float32 [2048, 1152], P(('dp', 'rep'), 'enc')
- grad_w_cnx: float32 [2048, 3072], P(('dp', 'rep'), 'enc')
- gradient_before_siglip: bfloat16 [32768, 1152], P(('dp', 'rep'), 'enc')
- gradient_before_convnext: bfloat16 [32768, 3072], P(('dp', 'rep'), 'enc')
The draws below stay inside these ranges and needn't reach their ends.
Inputs may be any that keep to these rules, and one draw needn't show every extreme that they name: `lengths`: every entry is 1, 2, 3 or 4; every row holds at least one entry equal to 4. `enc_of`: each row is a permutation of 0 .. 63. `owner_of`: each row is a permutation of 0 .. 63.
All inputs are finite; a program needn't handle non-finite values.
Results may differ from the reference program's by a relative error of at most 0.0049.
Values may be sent and summed in bfloat16 or wider, within the bound.
No kernel may reach another device: no remote copies, remote signals or barrier semaphores. Data moves between devices by JAX's collectives and lax.ppermute only.
A program may use at most 32 MiB of HBM per device.

```python
import math
import jax
import jax.numpy as jnp
from jax import lax

D = 2048
C_SIG = 1152
C_CNX = 3072
CAP = 4
TOKENS = 32768
N_DP = 64
N_REP = 2


def draw_lengths(key, part):
    key = jax.random.fold_in(key, 7)
    owners = N_DP * N_REP
    units = jax.random.randint(key, (owners, N_DP), 1, 5)
    longest = jax.random.randint(jax.random.fold_in(key, 1), (owners, 1), 0, N_DP)
    columns = lax.broadcasted_iota(jnp.int32, (owners, N_DP), 1)
    units = jnp.where(columns == longest, 4, units)
    return (units * (CAP // 4)).astype(jnp.int32)


def with_spikes(values, key, source, target, blocks, factor):
    owner, partner = [(jnp.arange(values.shape[position]) // (values.shape[position] // blocks)).reshape([-1 if axis == position else 1 for axis in range(values.ndim)]) for position in (source, target)]
    chosen = jax.random.permutation(key, blocks)[partner]
    strong = (owner == chosen) | (owner == (partner + blocks // 2) % blocks)
    return jnp.where(strong, factor * values, values)


def block_scale(key, shape, shards, low, largest):
    level = 1.0
    for axis_at, shards_of in shards:
        heights = jax.random.uniform(jax.random.fold_in(jax.random.fold_in(key, 6), axis_at), (shards_of,), jnp.float32, low / len(shards), largest / len(shards))
        level = level * jnp.repeat(jnp.exp(heights), shape[axis_at] // shards_of).reshape((-1,) + (1,) * (len(shape) - 1 - axis_at))
    return level


def scatter_about(key, extent, deviation, reach, shards=(), dtype=jnp.bfloat16):
    values = jax.random.normal(key, extent, jnp.float32) * deviation
    if len(shards) > 0:
        values = block_scale(key, extent, shards, -0.22, 0.18) * values
    return jnp.clip(values, min=-reach, max=reach).astype(dtype)


def noise_with(rng, extent, width, bound, shards, heavy, kind=jnp.bfloat16):
    entries = width * jax.random.normal(rng, extent, jnp.float32)
    if shards:
        entries = entries * block_scale(rng, extent, shards, -0.22, 0.18)
    return jnp.clip(with_spikes(entries, jax.random.fold_in(rng, 3), *heavy), -bound, bound).astype(kind)


def setup_inputs(seed: int = 0) -> dict:
    arg_keys = jax.random.split(jax.random.key(seed), 13)
    return {
        "feat_sig": scatter_about(arg_keys[0], (TOKENS, C_SIG), 1.0, 6.0, ((0, 128), (1, 8))),
        "feat_cnx": scatter_about(arg_keys[1], (TOKENS, C_CNX), 1.0, 6.0, ((0, 128), (1, 8))),
        "cotangent": noise_with(arg_keys[2], (TOKENS, D), 1.0, 24.0, ((0, 128), (1, 8)), (0, 1, 128, 5.5)),
        "w_sig": scatter_about(arg_keys[3], (D, C_SIG), (C_SIG + C_CNX) ** -0.5, 0.09375, ((1, 8),)),
        "w_cnx": scatter_about(arg_keys[4], (D, C_CNX), (C_SIG + C_CNX) ** -0.5, 0.09375, ((1, 8),)),
        "lengths": draw_lengths(jax.random.fold_in(arg_keys[12], 71), 0),
        "enc_of": jax.vmap(lambda own: jax.random.permutation(own, N_DP))(jax.random.split(arg_keys[6], (N_DP * N_REP))).reshape((N_DP * N_REP, N_DP)).astype(jnp.int32),
        "owner_of": jax.vmap(lambda own: jax.random.permutation(own, N_DP))(jax.random.split(arg_keys[7], (N_DP * N_REP))).reshape((N_DP * N_REP, N_DP)).astype(jnp.int32),
        "pre_sig": scatter_about(arg_keys[8], (TOKENS, C_SIG), 1.0, 6.0, ((0, 128), (1, 8))),
        "pre_cnx": scatter_about(arg_keys[9], (TOKENS, C_CNX), 1.0, 6.0, ((0, 128), (1, 8))),
        "gain_sig": jnp.clip(jnp.exp(math.log(2.0) - 1.3862944 * jax.random.uniform(arg_keys[10], (C_SIG,), jnp.float32) ** block_scale(arg_keys[10], (C_SIG,), ((0, 8),), -0.2, 0.2)), 0.5, 2.0),
        "gain_cnx": jnp.clip(jnp.exp(math.log(2.0) - 1.3862944 * jax.random.uniform(arg_keys[11], (C_CNX,), jnp.float32) ** block_scale(arg_keys[11], (C_CNX,), ((0, 8),), -0.2, 0.2)), 0.5, 2.0),
    }


EPS = 1e-06

def live_mask(lengths):
    owners, slots = lengths.shape
    spots = lax.broadcasted_iota(jnp.int32, (owners, slots, CAP), 2)
    return (spots < lengths[:, :, None]).reshape(owners * slots * CAP, 1)

def route(grad_rows, enc_of, owner_of):
    owners, slots = enc_of.shape
    inverse = jnp.argsort(enc_of, axis=1).astype(jnp.int32)
    blocks = lax.broadcasted_iota(jnp.int32, (owners, slots), 0)
    enc_dev = blocks // N_REP
    rep_index = blocks % N_REP
    source_owner = (owner_of * N_REP + rep_index).astype(jnp.int32)
    source_slot = inverse[source_owner, enc_dev]
    flat = (source_owner * slots + source_slot).reshape(-1).astype(jnp.int32)
    cells = grad_rows.reshape(owners * slots, CAP, grad_rows.shape[1])
    return cells[flat].reshape(owners * slots * CAP, grad_rows.shape[1])

def norm_back(pre, grad_in, gain):
    feature_width = pre.shape[-1]
    row_height = pre.astype(jnp.float32)
    hidden_mean = lax.optimization_barrier(jnp.sum(row_height, axis=-1, keepdims=True)) / feature_width
    var_h = lax.optimization_barrier(jnp.sum(row_height * row_height, axis=-1, keepdims=True)) / feature_width - hidden_mean * hidden_mean
    inverse_deviation = lax.rsqrt(var_h + EPS)
    normalized_input = (row_height - hidden_mean) * inverse_deviation
    scaled_gradient = grad_in.astype(jnp.float32) * gain
    gradient_mean = lax.optimization_barrier(jnp.sum(scaled_gradient, axis=-1, keepdims=True)) / feature_width
    gradient_product_mean = lax.optimization_barrier(jnp.sum(scaled_gradient * normalized_input, axis=-1, keepdims=True)) / feature_width
    return (inverse_deviation * (scaled_gradient - gradient_mean - normalized_input * gradient_product_mean)).astype(jnp.bfloat16)

def blocked_norm(pre, grad_in, gain, owners):
    feature_width = pre.shape[1]
    pre_blocks = pre.reshape(owners, -1, feature_width)
    grad_blocks = grad_in.reshape(owners, -1, feature_width)
    result = lax.map(lambda pair: norm_back(pair[0], pair[1], gain), (pre_blocks, grad_blocks))
    return result.reshape(-1, feature_width)

def reference(feat_sig, feat_cnx, cotangent, w_sig, w_cnx, lengths, enc_of, owner_of, pre_sig, pre_cnx, gain_sig, gain_cnx):
    owners = lengths.shape[0]
    live = live_mask(lengths)
    masked = jnp.where(live, cotangent, jnp.zeros_like(cotangent))
    back_sig = jnp.dot(masked, w_sig, preferred_element_type=jnp.float32).astype(jnp.bfloat16)
    back_cnx = jnp.dot(masked, w_cnx, preferred_element_type=jnp.float32).astype(jnp.bfloat16)
    scale = 1.0 / math.sqrt(TOKENS)
    grad_w_sig = jnp.dot(masked.T, feat_sig, preferred_element_type=jnp.float32) * scale
    grad_w_cnx = jnp.dot(masked.T, feat_cnx, preferred_element_type=jnp.float32) * scale
    dy_sig = route(back_sig, enc_of, owner_of)
    dy_cnx = route(back_cnx, enc_of, owner_of)
    gradient_before_siglip = blocked_norm(pre_sig, dy_sig, gain_sig, owners)
    gradient_before_convnext = blocked_norm(pre_cnx, dy_cnx, gain_cnx, owners)
    return (grad_w_sig, grad_w_cnx, gradient_before_siglip, gradient_before_convnext)
```

```python
import math

import jax
import jax.numpy as jnp
from jax import lax
from jax.sharding import Mesh
from jax.sharding import PartitionSpec as P

EPS = 1e-06
F32 = jnp.float32
BF16 = jnp.bfloat16


def shift(count, step):
    return [(i, (i + step) % count) for i in range(count)]


def broadcast_gather(block, axis):
    count = lax.axis_size(axis)
    copies = jnp.broadcast_to(block[None], (count,) + block.shape)
    return lax.all_to_all(copies, axis, 0, 0, tiled=True)


def reduce_stage(part, axis):
    count = lax.axis_size(axis)
    here = lax.axis_index(axis)
    rounded = part.astype(BF16)
    received = []
    for step in range(1, count):
        target = lax.rem(here + step, count)
        block = lax.dynamic_index_in_dim(rounded, target, 0, keepdims=False)
        received.append(lax.ppermute(block, axis, shift(count, step)))
    total = lax.dynamic_index_in_dim(part, here, 0, keepdims=False)
    for block in received:
        total = total + block.astype(F32)
    return total


def hand_on(blocks, axis):
    count = lax.axis_size(axis)
    return [blocks[0]] + [lax.ppermute(blocks[k], axis, shift(count, k)) for k in range(1, count)]


def pick(chosen, source):
    return jnp.dot(chosen.astype(BF16), source, preferred_element_type=F32).astype(BF16)


def shards(
    feat_sig,
    feat_cnx,
    cotangent,
    w_sig,
    w_cnx,
    lengths,
    enc_of,
    owner_of,
    pre_sig,
    pre_cnx,
    gain_sig,
    gain_cnx,
):
    slots = lengths.shape[1]
    rows, cols = cotangent.shape
    depth = rows // slots
    enc_count = lax.axis_size("enc")
    rep_count = lax.axis_size("rep")
    nx, nh, nl = (lax.axis_size(name) for name in ("x", "zh", "zl"))
    core = lax.axis_index("rep")
    swap = shift(rep_count, 1)

    features = jnp.concatenate([feat_cnx, feat_sig], axis=1)
    other_features = lax.ppermute(features, "rep", swap)
    live_t = lax.broadcasted_iota(jnp.int32, (slots, depth), 1) < lengths[0][:, None]
    live_t = live_t.reshape(1, rows)
    turned = jnp.where(live_t, cotangent.T, jnp.zeros((), BF16))
    piece = cols // (slots // enc_count) // rep_count
    turned = turned.reshape(slots // enc_count, rep_count, piece, rows)
    mine = lax.dynamic_index_in_dim(turned, core, 1, keepdims=False).reshape(cols // rep_count, rows)
    theirs = lax.dynamic_index_in_dim(turned, 1 - core, 1, keepdims=False).reshape(cols // rep_count, rows)
    theirs = lax.ppermute(theirs, "rep", swap)
    paired = jnp.stack([mine, theirs])
    all_paired = broadcast_gather(paired, "enc")

    hx, hh, hl = (lax.axis_index(name) for name in ("x", "zh", "zl"))
    token = lax.broadcasted_iota(jnp.int32, (slots, depth), 1)
    goal = enc_of[0]
    kx, kh, kl = (goal // (nh * nl) - hx) % nx, (goal // nl - hh) % nh, (goal - hl) % nl
    goal = (((kx * nh + kh) * nl + kl) * depth)[:, None] + token
    goal = jnp.where(token < lengths[0][:, None], goal, -1).reshape(1, rows)
    row = lax.broadcasted_iota(jnp.int32, (rows, rows), 0)
    column = lax.broadcasted_iota(jnp.int32, (rows, rows), 1)
    held = pick(row == goal, cotangent)
    held = jnp.concatenate(hand_on(jnp.split(held, nx), "x"))
    unit = row // depth
    unit = (unit % nx * nh + unit // nx % nh) * nl + unit // (nx * nh)
    held = pick(column == unit * depth + row % depth, held)
    held = hand_on(jnp.split(held, nl), "zl")
    held = [jnp.split(block, nh) for block in held]
    held = [jnp.concatenate([block[k] for block in held]) for k in range(nh)]
    held = jnp.concatenate(hand_on(held, "zh"))
    sender = owner_of[0]
    kx, kh, kl = (hx - sender // (nh * nl)) % nx, (hh - sender // nl) % nh, (hl - sender) % nl
    place = ((((kh * nl + kl) * nx + kx) * depth)[:, None] + token).reshape(rows, 1)
    routed = pick(column == place, held)
    routed, other_features = lax.optimization_barrier((routed, other_features))
    full = broadcast_gather(routed, "enc")

    parts = all_paired.reshape(enc_count, rep_count, cols // rep_count, rows)
    contract = (((1,), (0,)), ((), ()))
    half = enc_count * cols // rep_count
    partial = lax.dot_general(
        parts[:, 0].reshape(half, rows), features, contract, preferred_element_type=F32
    ) + lax.dot_general(
        parts[:, 1].reshape(half, rows), other_features, contract, preferred_element_type=F32
    )
    width = features.shape[1]
    total = reduce_stage(partial.reshape(nx, half // nx, width), "x")
    total = total.reshape(nh, nl, piece, width).transpose(1, 0, 2, 3).reshape(nl, nh * piece, width)
    total = reduce_stage(total, "zl")
    full, total = lax.optimization_barrier((full, total))
    total = reduce_stage(total.reshape(nh, piece, width), "zh")
    scale = 1.0 / math.sqrt(rows * nx * nh * nl * rep_count)
    total = total * scale
    split = feat_cnx.shape[1]

    full = full.transpose(1, 0, 2).reshape(rows, enc_count * cols)
    sums = []
    kept = []
    for weight, gain, pre in ((w_sig, gain_sig, pre_sig), (w_cnx, gain_cnx, pre_cnx)):
        dy = jnp.dot(full, weight, preferred_element_type=F32).astype(BF16)
        height = pre.astype(F32)
        scaled = dy.astype(F32) * gain
        kept.append((height, scaled, gain.shape[0] * enc_count))
        sums += [
            jnp.sum(height, axis=1),
            jnp.sum(height * height, axis=1),
            jnp.sum(scaled, axis=1),
            jnp.sum(scaled * height, axis=1),
        ]
    sums = jnp.sum(broadcast_gather(jnp.stack(sums), "enc").reshape(enc_count, 8, rows), axis=0)
    grads = []
    for index, (height, scaled, channels) in enumerate(kept):
        means = sums[index * 4 : index * 4 + 4] / channels
        mean = means[0]
        inverse = lax.rsqrt(means[1] - mean * mean + EPS)
        product = inverse * (means[3] - mean * means[2])
        grads.append(
            (
                inverse[:, None]
                * (scaled - means[2][:, None] - (height - mean[:, None]) * inverse[:, None] * product[:, None])
            ).astype(BF16)
        )
    return (total[:, split:], total[:, :split], grads[0], grads[1])


def solution(mesh):
    enc, dp, rep = mesh.devices.shape
    digit = round(dp ** (1 / 3))
    mesh = Mesh(
        mesh.devices.reshape(enc, dp // digit**2, digit, digit, rep), ("enc", "x", "zh", "zl", "rep")
    )
    owners = ("x", "zh", "zl", "rep")
    both = P(owners, "enc")
    in_specs = (
        both,
        both,
        both,
        P(None, "enc"),
        P(None, "enc"),
        P(owners, None),
        P(owners, None),
        P(owners, None),
        both,
        both,
        P("enc"),
        P("enc"),
    )
    return jax.shard_map(
        shards, mesh=mesh, in_specs=in_specs, out_specs=(both,) * 4, check_vma=False
    )
```

```python
import functools
import math

import jax
import jax.numpy as jnp
from jax import lax
from jax.experimental import pallas as pl
from jax.experimental.pallas import tpu as pltpu
from jax.sharding import Mesh
from jax.sharding import PartitionSpec as P

EPS = 1e-06
F32 = jnp.float32
BF16 = jnp.bfloat16
VMEM = pl.BlockSpec(memory_space=pltpu.VMEM)
SMEM = pl.BlockSpec(memory_space=pltpu.SMEM)


def shift(count, step):
    return [(i, (i + step) % count) for i in range(count)]


def broadcast_gather(block, axis):
    count = lax.axis_size(axis)
    copies = jnp.broadcast_to(block[None], (count,) + block.shape)
    return lax.all_to_all(copies, axis, 0, 0, tiled=True)


def exchange(blocks, axis):
    return lax.all_to_all(blocks, axis, 0, 0, tiled=True)


def hand_on(blocks, axis):
    count = lax.axis_size(axis)
    return [blocks[0]] + [lax.ppermute(blocks[k], axis, shift(count, k)) for k in range(1, count)]


def pick(chosen, source):
    return jnp.dot(chosen.astype(BF16), source, preferred_element_type=F32).astype(BF16)


def partial_kernel(here_ref, paired_ref, own_ref, other_ref, *outs):
    count = len(outs)
    rows = own_ref.shape[0]
    block = outs[0].shape[0]
    for k, out in enumerate(outs):
        target = lax.rem(here_ref[0] + k, count)
        start = pl.multiple_of(target * block, block)
        lhs = paired_ref[pl.ds(start, block), :]
        out[...] = (
            jnp.dot(lhs[:, :rows], own_ref[...], preferred_element_type=F32)
            + jnp.dot(lhs[:, rows:], other_ref[...], preferred_element_type=F32)
        ).astype(out.dtype)


def first_sum_kernel(nh, nl, piece, own_ref, *refs):
    out = refs[-1]
    for h in range(nh):
        for l in range(nl):
            at = pl.ds((h * nl + l) * piece, piece)
            total = own_ref[at, :]
            for ref in refs[:-1]:
                total += ref[at, :].astype(F32)
            out[l, pl.ds(h * piece, piece), :] = total.astype(BF16)


def sum_kernel(scale, split, parts_ref, *outs):
    total = parts_ref[0].astype(F32)
    for k in range(1, parts_ref.shape[0]):
        total += parts_ref[k].astype(F32)
    if split is None:
        outs[0][...] = total.astype(BF16)
    else:
        total *= scale
        outs[0][...] = total[:, :split]
        outs[1][...] = total[:, split:]


def shards(
    feat_sig,
    feat_cnx,
    cotangent,
    w_sig,
    w_cnx,
    lengths,
    enc_of,
    owner_of,
    pre_sig,
    pre_cnx,
    gain_sig,
    gain_cnx,
):
    slots = lengths.shape[1]
    rows, cols = cotangent.shape
    depth = rows // slots
    enc_count = lax.axis_size("enc")
    rep_count = lax.axis_size("rep")
    nx, nh, nl = (lax.axis_size(name) for name in ("x", "zh", "zl"))
    hx, hh = lax.axis_index("x"), lax.axis_index("zh")
    core = lax.axis_index("rep")
    swap = shift(rep_count, 1)

    token = lax.broadcasted_iota(jnp.int32, (slots, depth), 1)
    live = token < lengths[0][:, None]
    goal = jnp.where(live, (enc_of[0] * depth)[:, None] + token, -1).reshape(1, rows)
    row = lax.broadcasted_iota(jnp.int32, (rows, rows), 0)
    column = lax.broadcasted_iota(jnp.int32, (rows, rows), 1)
    held = pick(row == goal, cotangent)
    held = exchange(held.reshape(nx, rows // nx, cols), "x").reshape(rows, cols)
    line = lax.broadcasted_iota(jnp.int32, (rows, 1), 0)
    unit = line // depth
    unit = (unit % nx * nh + (unit // nx + hh) % nh) * nl + unit // (nx * nh)
    held = pick(column == unit * depth + line % depth, held)
    held = exchange(held.reshape(nl, rows // nl, cols), "zl")

    turned = jnp.where(live.reshape(1, rows), cotangent.T, jnp.zeros((), BF16))
    chips = slots // enc_count
    piece = cols // chips // rep_count
    turned = turned.reshape(chips, rep_count, piece, rows)
    mine = lax.dynamic_index_in_dim(turned, core, 1, keepdims=False).reshape(cols // rep_count, rows)
    theirs = lax.dynamic_index_in_dim(turned, 1 - core, 1, keepdims=False).reshape(cols // rep_count, rows)
    theirs = lax.ppermute(theirs, "rep", swap)
    paired = jnp.concatenate([mine, theirs], axis=1)
    paired, held = lax.optimization_barrier((paired, held))
    paired = broadcast_gather(paired, "enc")
    features = jnp.concatenate([feat_cnx, feat_sig], axis=1)
    other_features = lax.ppermute(features, "rep", swap)

    held = held.reshape(nl, nh, nx * depth, cols)
    held = [held[:, k].reshape(nl * nx * depth, cols) for k in range(nh)]
    held = jnp.concatenate(hand_on(held, "zh"))
    sender = owner_of[0]
    sx, kh, sl = sender // (nh * nl), (hh - sender // nl) % nh, sender % nl
    place = ((((kh * nl + sl) * nx + sx) * depth)[:, None] + token).reshape(rows, 1)
    routed = pick(column == place, held)
    routed, other_features = lax.optimization_barrier((routed, other_features))
    full = broadcast_gather(routed, "enc")

    half = enc_count * cols // rep_count
    width = features.shape[1]
    block = half // nx
    parts = pl.pallas_call(
        partial_kernel,
        out_shape=[
            jax.ShapeDtypeStruct((block, width), F32 if k == 0 else BF16) for k in range(nx)
        ],
        in_specs=[SMEM, VMEM, VMEM, VMEM],
        out_specs=[VMEM] * nx,
        compiler_params=pltpu.CompilerParams(vmem_limit_bytes=32 * 2**20),
        cost_estimate=pl.CostEstimate(
            flops=4 * half * rows * width, bytes_accessed=4 * half * width, transcendentals=0
        ),
        name="partial",
    )(hx.reshape(1), paired.reshape(half, rep_count * rows), features, other_features)
    parts = hand_on(parts, "x")
    total = pl.pallas_call(
        functools.partial(first_sum_kernel, nh, nl, piece),
        out_shape=jax.ShapeDtypeStruct((nl, nh * piece, width), BF16),
        in_specs=[VMEM] * nx,
        out_specs=VMEM,
        name="sum_x",
    )(*parts)
    full, total = lax.optimization_barrier((full, total))
    total = exchange(total, "zl")
    total = pl.pallas_call(
        functools.partial(sum_kernel, None, None),
        out_shape=[jax.ShapeDtypeStruct((nh * piece, width), BF16)],
        in_specs=[VMEM],
        out_specs=[VMEM],
        name="sum_zl",
    )(total)[0]
    total = exchange(total.reshape(nh, piece, width), "zh")

    full = full.transpose(1, 0, 2).reshape(rows, enc_count * cols)
    sums = []
    kept = []
    for weight, gain, pre in ((w_sig, gain_sig, pre_sig), (w_cnx, gain_cnx, pre_cnx)):
        dy = jnp.dot(full, weight, preferred_element_type=F32).astype(BF16)
        height = pre.astype(F32)
        scaled = dy.astype(F32) * gain
        kept.append((height, scaled, gain.shape[0] * enc_count))
        sums += [
            jnp.sum(height, axis=1),
            jnp.sum(height * height, axis=1),
            jnp.sum(scaled, axis=1),
            jnp.sum(scaled * height, axis=1),
        ]
    sums, total = lax.optimization_barrier((jnp.stack(sums), total))
    sums = jnp.sum(broadcast_gather(sums, "enc").reshape(enc_count, 8, rows), axis=0)
    split = feat_cnx.shape[1]
    grad_cnx, grad_sig = pl.pallas_call(
        functools.partial(sum_kernel, 1.0 / math.sqrt(rows * nx * nh * nl * rep_count), split),
        out_shape=[
            jax.ShapeDtypeStruct((piece, split), F32),
            jax.ShapeDtypeStruct((piece, width - split), F32),
        ],
        in_specs=[VMEM],
        out_specs=[VMEM, VMEM],
        name="sum_zh",
    )(total)
    grads = []
    for index, (height, scaled, channels) in enumerate(kept):
        means = sums[index * 4 : index * 4 + 4] / channels
        mean = means[0]
        inverse = lax.rsqrt(means[1] - mean * mean + EPS)
        product = inverse * (means[3] - mean * means[2])
        grads.append(
            (
                inverse[:, None]
                * (scaled - means[2][:, None] - (height - mean[:, None]) * inverse[:, None] * product[:, None])
            ).astype(BF16)
        )
    return (grad_sig, grad_cnx, grads[0], grads[1])


def solution(mesh):
    enc, dp, rep = mesh.devices.shape
    digit = round(dp ** (1 / 3))
    mesh = Mesh(
        mesh.devices.reshape(enc, dp // digit**2, digit, digit, rep), ("enc", "x", "zh", "zl", "rep")
    )
    owners = ("x", "zh", "zl", "rep")
    both = P(owners, "enc")
    in_specs = (
        both,
        both,
        both,
        P(None, "enc"),
        P(None, "enc"),
        P(owners, None),
        P(owners, None),
        P(owners, None),
        both,
        both,
        P("enc"),
        P("enc"),
    )
    return jax.shard_map(
        shards, mesh=mesh, in_specs=in_specs, out_specs=(both,) * 4, check_vma=False
    )
```

```python
import functools
import math

import jax
import jax.numpy as jnp
from jax import lax
from jax.experimental import pallas as pl
from jax.experimental.pallas import tpu as pltpu
from jax.sharding import Mesh
from jax.sharding import PartitionSpec as P

EPS = 1e-06
F32 = jnp.float32
BF16 = jnp.bfloat16
VMEM = pl.BlockSpec(memory_space=pltpu.VMEM)
SMEM = pl.BlockSpec(memory_space=pltpu.SMEM)


def shift(count, step):
    return [(i, (i + step) % count) for i in range(count)]


def broadcast_gather(block, axis):
    count = lax.axis_size(axis)
    copies = jnp.broadcast_to(block[None], (count,) + block.shape)
    return lax.all_to_all(copies, axis, 0, 0, tiled=True)


def exchange(blocks, axis):
    return lax.all_to_all(blocks, axis, 0, 0, tiled=True)


def hand_on(blocks, axis):
    count = lax.axis_size(axis)
    return [blocks[0]] + [lax.ppermute(blocks[k], axis, shift(count, k)) for k in range(1, count)]


def pick(chosen, source):
    return jnp.dot(chosen.astype(BF16), source, preferred_element_type=F32).astype(BF16)


def partial_kernel(here_ref, gathered_ref, own_ref, paired_ref, other_ref, *outs):
    count = len(outs)
    each = gathered_ref.shape[0] // count
    piece = gathered_ref.shape[2]
    for k, out in enumerate(outs):
        target = lax.rem(here_ref[0] + k, count)
        for j in range(each):
            at = target * each + j
            out[pl.ds(j * piece, piece), :] = (
                jnp.dot(gathered_ref[at, 0], own_ref[...], preferred_element_type=F32)
                + jnp.dot(paired_ref[at], other_ref[...], preferred_element_type=F32)
            ).astype(out.dtype)


def sum_x_kernel(own_ref, *refs):
    total = own_ref[...]
    for ref in refs[:-1]:
        total += ref[...].astype(F32)
    refs[-1][...] = total.astype(BF16)


def sum_z_kernel(scale, split, parts_ref, cnx_ref, sig_ref):
    total = parts_ref[0].astype(F32)
    for k in range(1, parts_ref.shape[0]):
        total += parts_ref[k].astype(F32)
    total *= scale
    cnx_ref[...] = total[:, :split]
    sig_ref[...] = total[:, split:]


def shards(
    feat_sig,
    feat_cnx,
    cotangent,
    w_sig,
    w_cnx,
    lengths,
    enc_of,
    owner_of,
    pre_sig,
    pre_cnx,
    gain_sig,
    gain_cnx,
):
    slots = lengths.shape[1]
    rows, cols = cotangent.shape
    depth = rows // slots
    enc_count = lax.axis_size("enc")
    rep_count = lax.axis_size("rep")
    nx, nz = lax.axis_size("x"), lax.axis_size("z")
    hx = lax.axis_index("x")
    core = lax.axis_index("rep")
    swap = shift(rep_count, 1)

    token = lax.broadcasted_iota(jnp.int32, (slots, depth), 1)
    live = (token < lengths[0][:, None]).reshape(1, rows)
    turned = jnp.where(live, cotangent.T, jnp.zeros((), BF16))
    chips = slots // enc_count
    piece = cols // chips // rep_count
    half = cols // rep_count
    turned = turned.reshape(chips, rep_count, piece, rows)
    turned = jnp.stack(
        [
            lax.dynamic_index_in_dim(turned, index, 1, keepdims=False).reshape(half, rows)
            for index in (core, 1 - core)
        ]
    )
    gathered = broadcast_gather(turned, "enc").reshape(enc_count, rep_count, half, rows)
    features = jnp.concatenate([feat_cnx, feat_sig], axis=1)
    other_features = lax.ppermute(features, "rep", swap)
    weight = jnp.concatenate([w_cnx, w_sig], axis=1)
    width = weight.shape[1]
    weight = weight.reshape(enc_count, chips, rep_count, piece, width)
    weight = jnp.stack(
        [
            lax.dynamic_index_in_dim(weight, index, 2, keepdims=False).reshape(enc_count, half, width)
            for index in (core, 1 - core)
        ],
        axis=1,
    ).reshape(enc_count * cols, width)
    gathered, other_features, weight = lax.optimization_barrier((gathered, other_features, weight))

    paired = lax.ppermute(gathered[:, 1], "rep", swap)

    row = lax.broadcasted_iota(jnp.int32, (rows, rows), 0)
    column = lax.broadcasted_iota(jnp.int32, (rows, rows), 1)
    line = lax.broadcasted_iota(jnp.int32, (rows, 1), 0)
    back = lax.dot_general(
        gathered.reshape(enc_count * cols, rows),
        weight,
        (((0,), (0,)), ((), ())),
        preferred_element_type=F32,
    ).astype(BF16)
    goal = ((enc_of[0] * depth)[:, None] + token).reshape(1, rows)
    held = pick(row == goal, back)
    held = exchange(held.reshape(nx, rows // nx, width), "x").reshape(rows, width)
    unit = line // depth
    unit = unit % nx * nz + unit // nx
    held = pick(column == unit * depth + line % depth, held)
    held = exchange(held.reshape(nz, rows // nz, width), "z").reshape(rows, width)
    sender = owner_of[0]
    place = (((sender % nz * nx + sender // nz) * depth)[:, None] + token).reshape(rows, 1)
    routed = pick(column == place, held)

    block = enc_count * half // nx
    parts = pl.pallas_call(
        partial_kernel,
        out_shape=[
            jax.ShapeDtypeStruct((block, width), F32 if k == 0 else BF16) for k in range(nx)
        ],
        in_specs=[SMEM, VMEM, VMEM, VMEM, VMEM],
        out_specs=[VMEM] * nx,
        compiler_params=pltpu.CompilerParams(vmem_limit_bytes=32 * 2**20),
        cost_estimate=pl.CostEstimate(
            flops=4 * enc_count * half * rows * width,
            bytes_accessed=4 * enc_count * half * width,
            transcendentals=0,
        ),
        name="partial",
    )(hx.reshape(1), gathered, features, paired, other_features)
    parts = hand_on(parts, "x")
    total = pl.pallas_call(
        sum_x_kernel,
        out_shape=jax.ShapeDtypeStruct((block, width), BF16),
        in_specs=[VMEM] * nx,
        out_specs=VMEM,
        name="sum_x",
    )(*parts)
    split = feat_cnx.shape[1]

    sums = []
    kept = []
    for dy, gain, pre in (
        (routed[:, split:], gain_sig, pre_sig),
        (routed[:, :split], gain_cnx, pre_cnx),
    ):
        height = pre.astype(F32)
        scaled = dy.astype(F32) * gain
        kept.append((height, scaled, gain.shape[0] * enc_count))
        sums += [
            jnp.sum(height, axis=1),
            jnp.sum(height * height, axis=1),
            jnp.sum(scaled, axis=1),
            jnp.sum(scaled * height, axis=1),
        ]
    sums = broadcast_gather(jnp.stack(sums), "enc")
    sums, total = lax.optimization_barrier((sums, total))
    sums = jnp.sum(sums.reshape(enc_count, 8, rows), axis=0)
    total = exchange(total.reshape(nz, block // nz, width), "z")
    grad_cnx, grad_sig = pl.pallas_call(
        functools.partial(sum_z_kernel, 1.0 / math.sqrt(rows * nx * nz * rep_count), split),
        out_shape=[
            jax.ShapeDtypeStruct((block // nz, split), F32),
            jax.ShapeDtypeStruct((block // nz, width - split), F32),
        ],
        in_specs=[VMEM],
        out_specs=[VMEM, VMEM],
        name="sum_z",
    )(total)
    grads = []
    for index, (height, scaled, channels) in enumerate(kept):
        means = sums[index * 4 : index * 4 + 4] / channels
        mean = means[0]
        inverse = lax.rsqrt(means[1] - mean * mean + EPS)
        product = inverse * (means[3] - mean * means[2])
        grads.append(
            (
                inverse[:, None]
                * (scaled - means[2][:, None] - (height - mean[:, None]) * inverse[:, None] * product[:, None])
            ).astype(BF16)
        )
    return (grad_sig, grad_cnx, grads[0], grads[1])


def solution(mesh):
    enc, dp, rep = mesh.devices.shape
    along_x = 4 if dp == 64 else 2
    mesh = Mesh(
        mesh.devices.reshape(enc, along_x, dp // along_x, rep), ("enc", "x", "z", "rep")
    )
    owners = ("x", "z", "rep")
    both = P(owners, "enc")
    in_specs = (
        both,
        both,
        both,
        P(None, "enc"),
        P(None, "enc"),
        P(owners, None),
        P(owners, None),
        P(owners, None),
        both,
        both,
        P("enc"),
        P("enc"),
    )
    return jax.shard_map(
        shards, mesh=mesh, in_specs=in_specs, out_specs=(both,) * 4, check_vma=False
    )
```

```python
import functools
import math

import jax
import jax.numpy as jnp
from jax import lax
from jax.experimental import pallas as pl
from jax.experimental.pallas import tpu as pltpu
from jax.sharding import Mesh
from jax.sharding import PartitionSpec as P

EPS = 1e-06
F32 = jnp.float32
BF16 = jnp.bfloat16
VMEM = pl.BlockSpec(memory_space=pltpu.VMEM)
SMEM = pl.BlockSpec(memory_space=pltpu.SMEM)


def shift(count, step):
    return [(i, (i + step) % count) for i in range(count)]


def broadcast_gather(block, axis):
    count = lax.axis_size(axis)
    copies = jnp.broadcast_to(block[None], (count,) + block.shape)
    return lax.all_to_all(copies, axis, 0, 0, tiled=True)


def exchange(blocks, axis):
    return lax.all_to_all(blocks, axis, 0, 0, tiled=True)


def hand_on(blocks, axis):
    count = lax.axis_size(axis)
    return [blocks[0]] + [lax.ppermute(blocks[k], axis, shift(count, k)) for k in range(1, count)]


def pick(chosen, source):
    return jnp.dot(chosen.astype(BF16), source, preferred_element_type=F32).astype(BF16)


def partial_kernel(here_ref, gathered_ref, own_ref, paired_ref, other_ref, *outs):
    count = len(outs)
    each = gathered_ref.shape[0] // count
    piece = gathered_ref.shape[2]
    for k, out in enumerate(outs):
        target = lax.rem(here_ref[0] + k, count)
        for j in range(each):
            at = target * each + j
            out[pl.ds(j * piece, piece), :] = (
                jnp.dot(gathered_ref[at, 0], own_ref[...], preferred_element_type=F32)
                + jnp.dot(paired_ref[at], other_ref[...], preferred_element_type=F32)
            ).astype(out.dtype)


def norm_kernel(channels, sums_ref, dy_ref, gain_ref, cnx_ref, sig_ref, cnx_out, sig_out):
    sums = sums_ref[...].T
    start = 0
    for index, (pre, out) in enumerate(((cnx_ref, cnx_out), (sig_ref, sig_out))):
        means = sums[:, index * 4 : index * 4 + 4] * (1.0 / channels[index])
        mean, grad_mean = means[:, 0:1], means[:, 2:3]
        inverse = lax.rsqrt(means[:, 1:2] - mean * mean + EPS)
        product = inverse * inverse * (means[:, 3:4] - mean * grad_mean)
        at = slice(start, start + pre.shape[1])
        scaled = dy_ref[:, at].astype(F32) * gain_ref[:, at]
        height = pre[...].astype(F32)
        out[...] = (inverse * (scaled - grad_mean - (height - mean) * product)).astype(BF16)
        start += pre.shape[1]


def shards(
    feat_sig,
    feat_cnx,
    cotangent,
    w_sig,
    w_cnx,
    lengths,
    enc_of,
    owner_of,
    pre_sig,
    pre_cnx,
    gain_sig,
    gain_cnx,
):
    slots = lengths.shape[1]
    rows, cols = cotangent.shape
    depth = rows // slots
    enc_count = lax.axis_size("enc")
    rep_count = lax.axis_size("rep")
    nx, nz = lax.axis_size("x"), lax.axis_size("z")
    hx = lax.axis_index("x")
    core = lax.axis_index("rep")
    swap = shift(rep_count, 1)

    token = lax.broadcasted_iota(jnp.int32, (slots, depth), 1)
    live = (token < lengths[0][:, None]).reshape(1, rows)
    turned = jnp.where(live, cotangent.T, jnp.zeros((), BF16))
    chips = slots // enc_count
    piece = cols // chips // rep_count
    half = cols // rep_count
    turned = turned.reshape(chips, rep_count, piece, rows)
    turned = jnp.stack(
        [
            lax.dynamic_index_in_dim(turned, index, 1, keepdims=False).reshape(half, rows)
            for index in (core, 1 - core)
        ]
    )
    gathered = broadcast_gather(turned, "enc").reshape(enc_count, rep_count, half, rows)
    features = jnp.concatenate([feat_cnx, feat_sig], axis=1)
    other_features = lax.ppermute(features, "rep", swap)
    weight = jnp.concatenate([w_cnx, w_sig], axis=1)
    width = weight.shape[1]
    weight = weight.reshape(enc_count, chips, rep_count, piece, width)
    weight = jnp.stack(
        [
            lax.dynamic_index_in_dim(weight, index, 2, keepdims=False).reshape(enc_count, half, width)
            for index in (core, 1 - core)
        ],
        axis=1,
    ).reshape(enc_count * cols, width)
    gathered, other_features, weight = lax.optimization_barrier((gathered, other_features, weight))

    paired = lax.ppermute(gathered[:, 1], "rep", swap)

    block = enc_count * half // nx
    parts = pl.pallas_call(
        partial_kernel,
        out_shape=[
            jax.ShapeDtypeStruct((block, width), F32 if k == 0 else BF16) for k in range(nx)
        ],
        in_specs=[SMEM, VMEM, VMEM, VMEM, VMEM],
        out_specs=[VMEM] * nx,
        compiler_params=pltpu.CompilerParams(vmem_limit_bytes=32 * 2**20),
        cost_estimate=pl.CostEstimate(
            flops=4 * enc_count * half * rows * width,
            bytes_accessed=4 * enc_count * half * width,
            transcendentals=0,
        ),
        name="partial",
    )(hx.reshape(1), gathered, features, paired, other_features)

    row = lax.broadcasted_iota(jnp.int32, (rows, rows), 0)
    column = lax.broadcasted_iota(jnp.int32, (rows, rows), 1)
    line = lax.broadcasted_iota(jnp.int32, (rows, 1), 0)
    back = lax.dot_general(
        gathered.reshape(enc_count * cols, rows),
        weight,
        (((0,), (0,)), ((), ())),
        preferred_element_type=F32,
    ).astype(BF16)
    goal = ((enc_of[0] * depth)[:, None] + token).reshape(1, rows)
    held = pick(row == goal, back)
    held = exchange(held.reshape(nx, rows // nx, width), "x").reshape(rows, width)
    unit = line // depth
    unit = unit % nx * nz + unit // nx
    held = pick(column == unit * depth + line % depth, held)
    held, parts = lax.optimization_barrier((held, parts))
    held = exchange(held.reshape(nz, rows // nz, width), "z").reshape(rows, width)
    sender = owner_of[0]
    place = (((sender % nz * nx + sender // nz) * depth)[:, None] + token).reshape(rows, 1)
    routed = pick(column == place, held)

    parts = hand_on(parts, "x")
    total = sum((part.astype(F32) for part in parts[1:]), parts[0]).astype(BF16)
    split = feat_cnx.shape[1]

    sums = []
    for dy, gain, pre in (
        (routed[:, :split], gain_cnx, pre_cnx),
        (routed[:, split:], gain_sig, pre_sig),
    ):
        height = pre.astype(F32)
        scaled = dy.astype(F32) * gain
        sums += [
            jnp.sum(height, axis=1),
            jnp.sum(height * height, axis=1),
            jnp.sum(scaled, axis=1),
            jnp.sum(scaled * height, axis=1),
        ]
    sums, total = lax.optimization_barrier((jnp.stack(sums), total))
    total = exchange(total.reshape(nz, block // nz, width), "z")
    sums = lax.psum(sums, "enc")
    before_cnx, before_sig = pl.pallas_call(
        functools.partial(
            norm_kernel, (gain_cnx.shape[0] * enc_count, gain_sig.shape[0] * enc_count)
        ),
        out_shape=[
            jax.ShapeDtypeStruct(pre_cnx.shape, BF16),
            jax.ShapeDtypeStruct(pre_sig.shape, BF16),
        ],
        in_specs=[VMEM] * 5,
        out_specs=[VMEM] * 2,
        cost_estimate=pl.CostEstimate(flops=1, bytes_accessed=1, transcendentals=0),
        name="norm",
    )(sums, routed, jnp.concatenate([gain_cnx, gain_sig])[None, :], pre_cnx, pre_sig)
    total = jnp.sum(total.astype(F32), axis=0) * (1.0 / math.sqrt(rows * nx * nz * rep_count))
    grad_cnx, grad_sig = total[:, :split], total[:, split:]
    return (grad_sig, grad_cnx, before_sig, before_cnx)


def solution(mesh):
    enc, dp, rep = mesh.devices.shape
    along_x = 4 if dp == 64 else 2
    mesh = Mesh(
        mesh.devices.reshape(enc, along_x, dp // along_x, rep), ("enc", "x", "z", "rep")
    )
    owners = ("x", "z", "rep")
    both = P(owners, "enc")
    in_specs = (
        both,
        both,
        both,
        P(None, "enc"),
        P(None, "enc"),
        P(owners, None),
        P(owners, None),
        P(owners, None),
        both,
        both,
        P("enc"),
        P("enc"),
    )
    return jax.shard_map(
        shards, mesh=mesh, in_specs=in_specs, out_specs=(both,) * 4, check_vma=False
    )
```

```python
import functools
import math

import jax
import jax.numpy as jnp
from jax import lax
from jax.experimental import pallas as pl
from jax.experimental.pallas import tpu as pltpu
from jax.sharding import Mesh
from jax.sharding import PartitionSpec as P

EPS = 1e-06
F32 = jnp.float32
BF16 = jnp.bfloat16
VMEM = pl.BlockSpec(memory_space=pltpu.VMEM)
SMEM = pl.BlockSpec(memory_space=pltpu.SMEM)


def shift(count, step):
    return [(i, (i + step) % count) for i in range(count)]


def exchange(blocks, axis):
    return lax.all_to_all(blocks, axis, 0, 0, tiled=True)


def hand_on(blocks, axis):
    count = lax.axis_size(axis)
    return [blocks[0]] + [lax.ppermute(blocks[k], axis, shift(count, k)) for k in range(1, count)]


def pick(chosen, source):
    return jnp.dot(chosen.astype(BF16), source, preferred_element_type=F32).astype(BF16)


def turn_kernel(pieces, core_ref, lengths_ref, cotangent_ref, out_ref, turned_ref):
    rows = cotangent_ref.shape[0]
    slots = lengths_ref.shape[1]
    depth = rows // slots
    lane = lax.broadcasted_iota(jnp.int32, (slots, rows), 1)
    slot = lax.broadcasted_iota(jnp.int32, (slots, rows), 0)
    spread = (lane >= slot * depth) & (lane < slot * depth + depth)
    first = jnp.broadcast_to(lengths_ref[...].astype(F32), (8, slots))
    limit = jnp.dot(first, spread.astype(F32), preferred_element_type=F32)[:1]
    token = lax.rem(lax.broadcasted_iota(jnp.int32, (1, rows), 1), depth).astype(F32)
    turned = cotangent_ref[...].astype(F32).T
    turned_ref[...] = jnp.where(token < limit, turned, 0.0).astype(BF16)
    halves = out_ref.shape[1]
    piece = out_ref.shape[2] // pieces
    for half in range(halves):
        source = lax.rem(core_ref[0] + half, halves)
        for k in range(pieces):
            start = pl.multiple_of((k * halves + source) * piece, piece)
            block = turned_ref[pl.ds(start, piece), :]
            for copy in range(out_ref.shape[0]):
                out_ref[copy, half, pl.ds(k * piece, piece), :] = block


def partial_kernel(here_ref, gathered_ref, own_ref, paired_ref, other_ref, *outs):
    count = len(outs)
    each = gathered_ref.shape[0] // count
    piece = gathered_ref.shape[2]
    for k, out in enumerate(outs):
        target = lax.rem(here_ref[0] + k, count)
        for j in range(each):
            at = target * each + j
            out[pl.ds(j * piece, piece), :] = (
                jnp.dot(gathered_ref[at, 0], own_ref[...], preferred_element_type=F32)
                + jnp.dot(paired_ref[at], other_ref[...], preferred_element_type=F32)
            ).astype(out.dtype)


def norm_kernel(channels, sums_ref, dy_ref, gain_ref, cnx_ref, sig_ref, cnx_out, sig_out):
    sums = sums_ref[...].T
    start = 0
    for index, (pre, out) in enumerate(((cnx_ref, cnx_out), (sig_ref, sig_out))):
        means = sums[:, index * 4 : index * 4 + 4] * (1.0 / channels[index])
        mean, grad_mean = means[:, 0:1], means[:, 2:3]
        inverse = lax.rsqrt(means[:, 1:2] - mean * mean + EPS)
        product = inverse * inverse * (means[:, 3:4] - mean * grad_mean)
        at = slice(start, start + pre.shape[1 - index])
        scaled = dy_ref[:, at].astype(F32) * gain_ref[:, at]
        height = pre[...].astype(F32)
        if index:
            height = height.T
        grad = inverse * (scaled - grad_mean - (height - mean) * product)
        out[...] = (grad.T if index else grad).astype(BF16)
        start += pre.shape[1]


def shards(
    feat_sig,
    feat_cnx,
    cotangent,
    w_sig,
    w_cnx,
    lengths,
    enc_of,
    owner_of,
    pre_sig,
    pre_cnx,
    gain_sig,
    gain_cnx,
):
    slots = lengths.shape[1]
    rows, cols = cotangent.shape
    depth = rows // slots
    enc_count = lax.axis_size("enc")
    rep_count = lax.axis_size("rep")
    nx, nz = lax.axis_size("x"), lax.axis_size("z")
    hx = lax.axis_index("x")
    core = lax.axis_index("rep")
    swap = shift(rep_count, 1)

    token = lax.broadcasted_iota(jnp.int32, (slots, depth), 1)
    chips = slots // enc_count
    piece = cols // chips // rep_count
    half = cols // rep_count
    copies = pl.pallas_call(
        functools.partial(turn_kernel, chips),
        out_shape=jax.ShapeDtypeStruct((enc_count, rep_count, half, rows), BF16),
        in_specs=[SMEM, VMEM, VMEM],
        out_specs=VMEM,
        scratch_shapes=[pltpu.VMEM((cols, rows), BF16)],
        name="turn",
    )(core.reshape(1), lengths, cotangent)
    gathered = exchange(copies, "enc")
    features = jnp.concatenate([feat_cnx, feat_sig], axis=1)
    other_features = lax.ppermute(features, "rep", swap)
    weight = jnp.concatenate([w_cnx, w_sig], axis=1)
    width = weight.shape[1]
    weight = weight.reshape(enc_count, chips, rep_count, piece, width)
    weight = jnp.stack(
        [
            lax.dynamic_index_in_dim(weight, index, 2, keepdims=False).reshape(enc_count, half, width)
            for index in (core, 1 - core)
        ],
        axis=1,
    ).reshape(enc_count * cols, width)
    gathered, other_features, weight = lax.optimization_barrier((gathered, other_features, weight))

    paired = lax.ppermute(gathered[:, 1], "rep", swap)

    block = enc_count * half // nx
    parts = pl.pallas_call(
        partial_kernel,
        out_shape=[
            jax.ShapeDtypeStruct((block, width), F32 if k == 0 else BF16) for k in range(nx)
        ],
        in_specs=[SMEM, VMEM, VMEM, VMEM, VMEM],
        out_specs=[VMEM] * nx,
        compiler_params=pltpu.CompilerParams(vmem_limit_bytes=32 * 2**20),
        cost_estimate=pl.CostEstimate(
            flops=4 * enc_count * half * rows * width,
            bytes_accessed=4 * enc_count * half * width,
            transcendentals=0,
        ),
        name="partial",
    )(hx.reshape(1), gathered, features, paired, other_features)

    row = lax.broadcasted_iota(jnp.int32, (rows, rows), 0)
    column = lax.broadcasted_iota(jnp.int32, (rows, rows), 1)
    back = lax.dot_general(
        gathered.reshape(enc_count * cols, rows),
        weight,
        (((0,), (0,)), ((), ())),
        preferred_element_type=F32,
    ).astype(BF16)
    goal = ((enc_of[0] * depth)[:, None] + token).reshape(1, rows)
    held = pick(row == goal, back).reshape(slots, depth, width)
    held = exchange(held, ("x", "z")).reshape(rows, width)
    place = ((owner_of[0] * depth)[:, None] + token).reshape(rows, 1)
    routed = pick(column == place, held)

    parts = hand_on(parts, "x")
    total = sum((part.astype(F32) for part in parts[1:]), parts[0]).astype(BF16)
    split = feat_cnx.shape[1]

    sums = []
    for dy, gain, pre in (
        (routed[:, :split], gain_cnx, pre_cnx),
        (routed[:, split:], gain_sig, pre_sig),
    ):
        height = pre.astype(F32)
        scaled = dy.astype(F32) * gain
        sums += [
            jnp.sum(height, axis=1),
            jnp.sum(height * height, axis=1),
            jnp.sum(scaled, axis=1),
            jnp.sum(scaled * height, axis=1),
        ]
    sums, total = lax.optimization_barrier((jnp.stack(sums), total))
    total = exchange(total.reshape(nz, block // nz, width), "z")
    sums = lax.psum(sums, "enc")
    before_cnx, before_sig = pl.pallas_call(
        functools.partial(
            norm_kernel, (gain_cnx.shape[0] * enc_count, gain_sig.shape[0] * enc_count)
        ),
        out_shape=[
            jax.ShapeDtypeStruct(pre_cnx.shape, BF16),
            jax.ShapeDtypeStruct(pre_sig.shape[::-1], BF16),
        ],
        in_specs=[VMEM] * 5,
        out_specs=[VMEM] * 2,
        cost_estimate=pl.CostEstimate(flops=1, bytes_accessed=1, transcendentals=0),
        name="norm",
    )(sums, routed, jnp.concatenate([gain_cnx, gain_sig])[None, :], pre_cnx, pre_sig.T)
    scale = 1.0 / math.sqrt(rows * nx * nz * rep_count)
    grad_cnx = jnp.sum(total[:, :, :split].astype(F32), axis=0) * scale
    grad_sig = jnp.sum(total[:, :, split:].astype(F32), axis=0) * scale
    return (grad_sig, grad_cnx, before_sig.T, before_cnx)


def solution(mesh):
    enc, dp, rep = mesh.devices.shape
    along_x = 4 if dp == 64 else 2
    mesh = Mesh(
        mesh.devices.reshape(enc, along_x, dp // along_x, rep), ("enc", "x", "z", "rep")
    )
    owners = ("x", "z", "rep")
    both = P(owners, "enc")
    in_specs = (
        both,
        both,
        both,
        P(None, "enc"),
        P(None, "enc"),
        P(owners, None),
        P(owners, None),
        P(owners, None),
        both,
        both,
        P("enc"),
        P("enc"),
    )
    return jax.shard_map(
        shards, mesh=mesh, in_specs=in_specs, out_specs=(both,) * 4, check_vma=False
    )
```

```python
import functools
import math

import jax
import jax.numpy as jnp
from jax import lax
from jax.experimental import pallas as pl
from jax.experimental.pallas import tpu as pltpu
from jax.sharding import Mesh
from jax.sharding import PartitionSpec as P

EPS = 1e-06
F32 = jnp.float32
BF16 = jnp.bfloat16
VMEM = pl.BlockSpec(memory_space=pltpu.VMEM)
SMEM = pl.BlockSpec(memory_space=pltpu.SMEM)


def shift(count, step):
    return [(i, (i + step) % count) for i in range(count)]


def exchange(blocks, axis):
    return lax.all_to_all(blocks, axis, 0, 0, tiled=True)


def hand_on(blocks, axis):
    count = lax.axis_size(axis)
    order = sorted(range(1, count), key=lambda k: -min(k, count - k))
    got = {k: lax.ppermute(blocks[k], axis, shift(count, k)) for k in order}
    return [blocks[0]] + [got[k] for k in range(1, count)]


def pick(chosen, source):
    return jnp.dot(chosen.astype(BF16), source, preferred_element_type=F32).astype(BF16)


def turn_kernel(pieces, core_ref, lengths_ref, cotangent_ref, out_ref, turned_ref):
    rows = cotangent_ref.shape[0]
    slots = lengths_ref.shape[1]
    depth = rows // slots
    lane = lax.broadcasted_iota(jnp.int32, (slots, rows), 1)
    slot = lax.broadcasted_iota(jnp.int32, (slots, rows), 0)
    spread = (lane >= slot * depth) & (lane < slot * depth + depth)
    first = jnp.broadcast_to(lengths_ref[...].astype(F32), (8, slots))
    limit = jnp.dot(first, spread.astype(F32), preferred_element_type=F32)[:1]
    token = lax.rem(lax.broadcasted_iota(jnp.int32, (1, rows), 1), depth).astype(F32)
    turned = cotangent_ref[...].astype(F32).T
    turned_ref[...] = jnp.where(token < limit, turned, 0.0).astype(BF16)
    halves = out_ref.shape[1]
    piece = out_ref.shape[2] // pieces
    for half in range(halves):
        source = lax.rem(core_ref[0] + half, halves)
        for k in range(pieces):
            start = pl.multiple_of((k * halves + source) * piece, piece)
            block = turned_ref[pl.ds(start, piece), :]
            for copy in range(out_ref.shape[0]):
                out_ref[copy, half, pl.ds(k * piece, piece), :] = block


def partial_kernel(here_ref, gathered_ref, own_ref, paired_ref, other_ref, *outs):
    count = len(outs)
    each = gathered_ref.shape[0] // count
    piece = gathered_ref.shape[2]
    main = outs[0].shape[1]
    rest = own_ref.shape[1] - main
    block = each * piece
    turned = (((0,), (1,)), ((), ()))
    own_rest = own_ref[:, main:]
    other_rest = other_ref[:, main:]
    for k, out in enumerate(outs):
        target = lax.rem(here_ref[0] + k, count)
        for j in range(each):
            at = target * each + j
            mine = gathered_ref[at, 0]
            theirs = paired_ref[at]
            out[pl.ds(j * piece, piece), :] = (
                jnp.dot(mine, own_ref[:, :main], preferred_element_type=F32)
                + jnp.dot(theirs, other_ref[:, :main], preferred_element_type=F32)
            ).astype(out.dtype)
            out[pl.ds(block, rest), pl.ds(j * piece, piece)] = (
                lax.dot_general(own_rest, mine, turned, preferred_element_type=F32)
                + lax.dot_general(other_rest, theirs, turned, preferred_element_type=F32)
            ).astype(out.dtype)
        out[pl.ds(block, rest), pl.ds(block, main - block)] = jnp.zeros(
            (rest, main - block), out.dtype
        )


def sum_x_kernel(own_ref, *refs):
    out = refs[-1]
    block = out.shape[0]
    main = own_ref.shape[1]
    total = own_ref[...]
    for ref in refs[:-1]:
        total += ref[...].astype(F32)
    out[:, :main] = total[:block].astype(BF16)
    out[:, main:] = total[block:, :block].T.astype(BF16)


def norm_kernel(channels, sums_ref, dy_ref, gain_ref, cnx_ref, sig_ref, cnx_out, sig_out):
    sums = sums_ref[...].T
    start = 0
    for index, (pre, out) in enumerate(((cnx_ref, cnx_out), (sig_ref, sig_out))):
        means = sums[:, index * 4 : index * 4 + 4] * (1.0 / channels[index])
        mean, grad_mean = means[:, 0:1], means[:, 2:3]
        inverse = lax.rsqrt(means[:, 1:2] - mean * mean + EPS)
        product = inverse * inverse * (means[:, 3:4] - mean * grad_mean)
        at = slice(start, start + pre.shape[1 - index])
        scaled = dy_ref[:, at].astype(F32) * gain_ref[:, at]
        height = pre[...].astype(F32)
        if index:
            height = height.T
        grad = inverse * (scaled - grad_mean - (height - mean) * product)
        out[...] = (grad.T if index else grad).astype(BF16)
        start += pre.shape[1]


def shards(
    feat_sig,
    feat_cnx,
    cotangent,
    w_sig,
    w_cnx,
    lengths,
    enc_of,
    owner_of,
    pre_sig,
    pre_cnx,
    gain_sig,
    gain_cnx,
):
    slots = lengths.shape[1]
    rows, cols = cotangent.shape
    depth = rows // slots
    enc_count = lax.axis_size("enc")
    rep_count = lax.axis_size("rep")
    nx, nz = lax.axis_size("x"), lax.axis_size("z")
    hx = lax.axis_index("x")
    core = lax.axis_index("rep")
    swap = shift(rep_count, 1)

    token = lax.broadcasted_iota(jnp.int32, (slots, depth), 1)
    chips = slots // enc_count
    piece = cols // chips // rep_count
    half = cols // rep_count
    copies = pl.pallas_call(
        functools.partial(turn_kernel, chips),
        out_shape=jax.ShapeDtypeStruct((enc_count, rep_count, half, rows), BF16),
        in_specs=[SMEM, VMEM, VMEM],
        out_specs=VMEM,
        scratch_shapes=[pltpu.VMEM((cols, rows), BF16)],
        name="turn",
    )(core.reshape(1), lengths, cotangent)
    gathered = exchange(copies, "enc")
    features = jnp.concatenate([feat_cnx, feat_sig], axis=1)
    other_features = lax.ppermute(features, "rep", swap)
    weight = jnp.concatenate([w_cnx, w_sig], axis=1)
    width = weight.shape[1]
    weight = weight.reshape(enc_count, chips, rep_count, piece, width)
    weight = jnp.stack(
        [
            lax.dynamic_index_in_dim(weight, index, 2, keepdims=False).reshape(enc_count, half, width)
            for index in (core, 1 - core)
        ],
        axis=1,
    ).reshape(enc_count * cols, width)
    gathered, other_features, weight = lax.optimization_barrier((gathered, other_features, weight))

    paired = lax.ppermute(gathered[:, 1], "rep", swap)

    row = lax.broadcasted_iota(jnp.int32, (rows, rows), 0)
    column = lax.broadcasted_iota(jnp.int32, (rows, rows), 1)
    back = lax.dot_general(
        gathered.reshape(enc_count * cols, rows),
        weight,
        (((0,), (0,)), ((), ())),
        preferred_element_type=F32,
    ).astype(BF16)
    goal = ((enc_of[0] * depth)[:, None] + token).reshape(1, rows)
    held = pick(row == goal, back).reshape(slots, depth, width)
    held, paired = lax.optimization_barrier((held, paired))
    held = exchange(held, ("x", "z")).reshape(rows, width)
    place = ((owner_of[0] * depth)[:, None] + token).reshape(rows, 1)
    routed = pick(column == place, held)

    block = enc_count * half // nx
    main = width // 128 * 128
    tall = block + width - main
    parts = pl.pallas_call(
        partial_kernel,
        out_shape=[
            jax.ShapeDtypeStruct((tall, main), F32 if k == 0 else BF16) for k in range(nx)
        ],
        in_specs=[SMEM, VMEM, VMEM, VMEM, VMEM],
        out_specs=[VMEM] * nx,
        compiler_params=pltpu.CompilerParams(vmem_limit_bytes=32 * 2**20),
        cost_estimate=pl.CostEstimate(
            flops=4 * enc_count * half * rows * width,
            bytes_accessed=4 * enc_count * half * width,
            transcendentals=0,
        ),
        name="partial",
    )(hx.reshape(1), gathered, features, paired, other_features)
    parts = hand_on(parts, "x")
    total = pl.pallas_call(
        sum_x_kernel,
        out_shape=jax.ShapeDtypeStruct((block, width), BF16),
        in_specs=[VMEM] * nx,
        out_specs=VMEM,
        name="sum_x",
    )(*parts)
    split = feat_cnx.shape[1]

    sums = []
    for dy, gain, pre in (
        (routed[:, :split], gain_cnx, pre_cnx),
        (routed[:, split:], gain_sig, pre_sig),
    ):
        height = pre.astype(F32)
        scaled = dy.astype(F32) * gain
        sums += [
            jnp.sum(height, axis=1),
            jnp.sum(height * height, axis=1),
            jnp.sum(scaled, axis=1),
            jnp.sum(scaled * height, axis=1),
        ]
    sums, total = lax.optimization_barrier((jnp.stack(sums), total))
    total = exchange(total.reshape(nz, block // nz, width), "z")
    sums = lax.psum(sums, "enc")
    before_cnx, before_sig = pl.pallas_call(
        functools.partial(
            norm_kernel, (gain_cnx.shape[0] * enc_count, gain_sig.shape[0] * enc_count)
        ),
        out_shape=[
            jax.ShapeDtypeStruct(pre_cnx.shape, BF16),
            jax.ShapeDtypeStruct(pre_sig.shape[::-1], BF16),
        ],
        in_specs=[VMEM] * 5,
        out_specs=[VMEM] * 2,
        cost_estimate=pl.CostEstimate(flops=1, bytes_accessed=1, transcendentals=0),
        name="norm",
    )(sums, routed, jnp.concatenate([gain_cnx, gain_sig])[None, :], pre_cnx, pre_sig.T)
    scale = 1.0 / math.sqrt(rows * nx * nz * rep_count)
    grad_cnx = jnp.sum(total[:, :, :split].astype(F32), axis=0) * scale
    grad_sig = jnp.sum(total[:, :, split:].astype(F32), axis=0) * scale
    return (grad_sig, grad_cnx, before_sig.T, before_cnx)


def solution(mesh):
    enc, dp, rep = mesh.devices.shape
    along_x = 4 if dp == 64 else 2
    mesh = Mesh(
        mesh.devices.reshape(enc, along_x, dp // along_x, rep), ("enc", "x", "z", "rep")
    )
    owners = ("x", "z", "rep")
    both = P(owners, "enc")
    in_specs = (
        both,
        both,
        both,
        P(None, "enc"),
        P(None, "enc"),
        P(owners, None),
        P(owners, None),
        P(owners, None),
        both,
        both,
        P("enc"),
        P("enc"),
    )
    return jax.shard_map(
        shards, mesh=mesh, in_specs=in_specs, out_specs=(both,) * 4, check_vma=False
    )
```

```python
import functools
import math

import jax
import jax.numpy as jnp
from jax import lax
from jax.experimental import pallas as pl
from jax.experimental.pallas import tpu as pltpu
from jax.sharding import Mesh
from jax.sharding import PartitionSpec as P

EPS = 1e-06
F32 = jnp.float32
BF16 = jnp.bfloat16
VMEM = pl.BlockSpec(memory_space=pltpu.VMEM)
SMEM = pl.BlockSpec(memory_space=pltpu.SMEM)


def shift(count, step):
    return [(i, (i + step) % count) for i in range(count)]


def exchange(blocks, axis):
    return lax.all_to_all(blocks, axis, 0, 0, tiled=True)


def pick(chosen, source):
    return jnp.dot(chosen.astype(BF16), source, preferred_element_type=F32).astype(BF16)


def turn_kernel(pieces, core_ref, lengths_ref, cotangent_ref, out_ref, turned_ref):
    rows = cotangent_ref.shape[0]
    slots = lengths_ref.shape[1]
    depth = rows // slots
    lane = lax.broadcasted_iota(jnp.int32, (slots, rows), 1)
    slot = lax.broadcasted_iota(jnp.int32, (slots, rows), 0)
    spread = (lane >= slot * depth) & (lane < slot * depth + depth)
    first = jnp.broadcast_to(lengths_ref[...].astype(F32), (8, slots))
    limit = jnp.dot(first, spread.astype(F32), preferred_element_type=F32)[:1]
    token = lax.rem(lax.broadcasted_iota(jnp.int32, (1, rows), 1), depth).astype(F32)
    turned = cotangent_ref[...].astype(F32).T
    turned_ref[...] = jnp.where(token < limit, turned, 0.0).astype(BF16)
    halves = out_ref.shape[1]
    piece = out_ref.shape[2] // pieces
    for half in range(halves):
        source = lax.rem(core_ref[0] + half, halves)
        for k in range(pieces):
            start = pl.multiple_of((k * halves + source) * piece, piece)
            block = turned_ref[pl.ds(start, piece), :]
            for copy in range(out_ref.shape[0]):
                out_ref[copy, half, pl.ds(k * piece, piece), :] = block


def partial_kernel(count, steps, here_ref, gathered_ref, own_ref, paired_ref, other_ref, *outs):
    each = gathered_ref.shape[0] // count
    piece = gathered_ref.shape[2]
    main = outs[0].shape[1]
    rest = own_ref.shape[1] - main
    block = each * piece
    turned = (((0,), (1,)), ((), ()))
    own_rest = own_ref[:, main:]
    other_rest = other_ref[:, main:]
    for k, out in zip(steps, outs):
        target = lax.rem(here_ref[0] + k, count)
        for j in range(each):
            at = target * each + j
            mine = gathered_ref[at, 0]
            theirs = paired_ref[at]
            out[pl.ds(j * piece, piece), :] = (
                jnp.dot(mine, own_ref[:, :main], preferred_element_type=F32)
                + jnp.dot(theirs, other_ref[:, :main], preferred_element_type=F32)
            ).astype(out.dtype)
            out[pl.ds(block, rest), pl.ds(j * piece, piece)] = (
                lax.dot_general(own_rest, mine, turned, preferred_element_type=F32)
                + lax.dot_general(other_rest, theirs, turned, preferred_element_type=F32)
            ).astype(out.dtype)
        out[pl.ds(block, rest), pl.ds(block, main - block)] = jnp.zeros(
            (rest, main - block), out.dtype
        )


def norm_kernel(channels, sums_ref, dy_ref, gain_ref, cnx_ref, sig_ref, cnx_out, sig_out):
    sums = sums_ref[...].T
    start = 0
    for index, (pre, out) in enumerate(((cnx_ref, cnx_out), (sig_ref, sig_out))):
        means = sums[:, index * 4 : index * 4 + 4] * (1.0 / channels[index])
        mean, grad_mean = means[:, 0:1], means[:, 2:3]
        inverse = lax.rsqrt(means[:, 1:2] - mean * mean + EPS)
        product = inverse * inverse * (means[:, 3:4] - mean * grad_mean)
        at = slice(start, start + pre.shape[1 - index])
        scaled = dy_ref[:, at].astype(F32) * gain_ref[:, at]
        height = pre[...].astype(F32)
        if index:
            height = height.T
        grad = inverse * (scaled - grad_mean - (height - mean) * product)
        out[...] = (grad.T if index else grad).astype(BF16)
        start += pre.shape[1]


def shards(
    feat_sig,
    feat_cnx,
    cotangent,
    w_sig,
    w_cnx,
    lengths,
    enc_of,
    owner_of,
    pre_sig,
    pre_cnx,
    gain_sig,
    gain_cnx,
):
    slots = lengths.shape[1]
    rows, cols = cotangent.shape
    depth = rows // slots
    enc_count = lax.axis_size("enc")
    rep_count = lax.axis_size("rep")
    nx, nz = lax.axis_size("x"), lax.axis_size("z")
    hx = lax.axis_index("x")
    core = lax.axis_index("rep")
    swap = shift(rep_count, 1)

    token = lax.broadcasted_iota(jnp.int32, (slots, depth), 1)
    chips = slots // enc_count
    piece = cols // chips // rep_count
    half = cols // rep_count
    copies = pl.pallas_call(
        functools.partial(turn_kernel, chips),
        out_shape=jax.ShapeDtypeStruct((enc_count, rep_count, half, rows), BF16),
        in_specs=[SMEM, VMEM, VMEM],
        out_specs=VMEM,
        scratch_shapes=[pltpu.VMEM((cols, rows), BF16)],
        name="turn",
    )(core.reshape(1), lengths, cotangent)
    gathered = exchange(copies, "enc")
    features = jnp.concatenate([feat_cnx, feat_sig], axis=1)
    other_features = lax.ppermute(features, "rep", swap)
    weight = jnp.concatenate([w_cnx, w_sig], axis=1)
    width = weight.shape[1]
    weight = weight.reshape(enc_count, chips, rep_count, piece, width)
    weight = jnp.stack(
        [
            lax.dynamic_index_in_dim(weight, index, 2, keepdims=False).reshape(enc_count, half, width)
            for index in (core, 1 - core)
        ],
        axis=1,
    ).reshape(enc_count * cols, width)
    gains = jnp.concatenate([gain_cnx, gain_sig])[None, :]
    gathered, other_features, weight, gains = lax.optimization_barrier(
        (gathered, other_features, weight, gains)
    )

    paired = lax.ppermute(gathered[:, 1], "rep", swap)

    block = enc_count * half // nx
    main = width // 128 * 128
    tall = block + width - main

    def multiply(steps):
        return list(
            pl.pallas_call(
                functools.partial(partial_kernel, nx, steps),
                out_shape=[
                    jax.ShapeDtypeStruct((tall, main), BF16 if k else F32) for k in steps
                ],
                in_specs=[SMEM, VMEM, VMEM, VMEM, VMEM],
                out_specs=[VMEM] * len(steps),
                compiler_params=pltpu.CompilerParams(vmem_limit_bytes=32 * 2**20),
                cost_estimate=pl.CostEstimate(
                    flops=4 * block * len(steps) * rows * width,
                    bytes_accessed=4 * block * len(steps) * width,
                    transcendentals=0,
                ),
                name="partial",
            )(hx.reshape(1), gathered, features, paired, other_features)
        )

    far = nx // 2
    (far_part,) = multiply([far])
    far_got = lax.ppermute(far_part, "x", shift(nx, far))

    row = lax.broadcasted_iota(jnp.int32, (rows, rows), 0)
    column = lax.broadcasted_iota(jnp.int32, (rows, rows), 1)
    back = lax.dot_general(
        gathered.reshape(enc_count * cols, rows),
        weight,
        (((0,), (0,)), ((), ())),
        preferred_element_type=F32,
    ).astype(BF16)
    goal = ((enc_of[0] * depth)[:, None] + token).reshape(1, rows)
    held = pick(row == goal, back).reshape(slots, depth, width)
    held, far_part = lax.optimization_barrier((held, far_part))
    held = exchange(held, ("x", "z")).reshape(rows, width)
    place = ((owner_of[0] * depth)[:, None] + token).reshape(rows, 1)
    routed = pick(column == place, held)

    parts = multiply([k for k in range(nx) if k != far])
    parts.insert(far, far_part)
    parts = [
        far_got if k == far else lax.ppermute(part, "x", shift(nx, k)) if k else part
        for k, part in enumerate(parts)
    ]
    total = sum((part.astype(F32) for part in parts[1:]), parts[0]).astype(BF16)
    total = jnp.concatenate([total[:block], total[block:, :block].T], axis=1)
    split = feat_cnx.shape[1]

    sums = []
    for dy, gain, pre in (
        (routed[:, :split], gain_cnx, pre_cnx),
        (routed[:, split:], gain_sig, pre_sig),
    ):
        height = pre.astype(F32)
        scaled = dy.astype(F32) * gain
        sums += [
            jnp.sum(height, axis=1),
            jnp.sum(height * height, axis=1),
            jnp.sum(scaled, axis=1),
            jnp.sum(scaled * height, axis=1),
        ]
    sums, total = lax.optimization_barrier((jnp.stack(sums), total))
    total = exchange(total.reshape(nz, block // nz, width), "z")
    sums = lax.psum(sums, "enc")
    before_cnx, before_sig = pl.pallas_call(
        functools.partial(
            norm_kernel, (gain_cnx.shape[0] * enc_count, gain_sig.shape[0] * enc_count)
        ),
        out_shape=[
            jax.ShapeDtypeStruct(pre_cnx.shape, BF16),
            jax.ShapeDtypeStruct(pre_sig.shape[::-1], BF16),
        ],
        in_specs=[VMEM] * 5,
        out_specs=[VMEM] * 2,
        cost_estimate=pl.CostEstimate(flops=1, bytes_accessed=1, transcendentals=0),
        name="norm",
    )(sums, routed, gains, pre_cnx, pre_sig.T)
    scale = 1.0 / math.sqrt(rows * nx * nz * rep_count)
    grad_cnx = jnp.sum(total[:, :, :split].astype(F32), axis=0) * scale
    grad_sig = jnp.sum(total[:, :, split:].astype(F32), axis=0) * scale
    return (grad_sig, grad_cnx, before_sig.T, before_cnx)


def solution(mesh):
    enc, dp, rep = mesh.devices.shape
    along_x = 4 if dp == 64 else 2
    mesh = Mesh(
        mesh.devices.reshape(enc, along_x, dp // along_x, rep), ("enc", "x", "z", "rep")
    )
    owners = ("x", "z", "rep")
    both = P(owners, "enc")
    in_specs = (
        both,
        both,
        both,
        P(None, "enc"),
        P(None, "enc"),
        P(owners, None),
        P(owners, None),
        P(owners, None),
        both,
        both,
        P("enc"),
        P("enc"),
    )
    return jax.shard_map(
        shards, mesh=mesh, in_specs=in_specs, out_specs=(both,) * 4, check_vma=False
    )
```

```python
import functools
import math

import jax
import jax.numpy as jnp
from jax import lax
from jax.experimental import pallas as pl
from jax.experimental.pallas import tpu as pltpu
from jax.sharding import Mesh
from jax.sharding import PartitionSpec as P

EPS = 1e-06
F32 = jnp.float32
BF16 = jnp.bfloat16
VMEM = pl.BlockSpec(memory_space=pltpu.VMEM)
SMEM = pl.BlockSpec(memory_space=pltpu.SMEM)


def shift(count, step):
    return [(i, (i + step) % count) for i in range(count)]


def exchange(blocks, axis):
    return lax.all_to_all(blocks, axis, 0, 0, tiled=True)


def pick(chosen, source):
    return jnp.dot(chosen.astype(BF16), source, preferred_element_type=F32).astype(BF16)


def turn_kernel(pieces, core_ref, lengths_ref, cotangent_ref, out_ref, turned_ref):
    rows = cotangent_ref.shape[0]
    slots = lengths_ref.shape[1]
    depth = rows // slots
    lane = lax.broadcasted_iota(jnp.int32, (slots, rows), 1)
    slot = lax.broadcasted_iota(jnp.int32, (slots, rows), 0)
    spread = (lane >= slot * depth) & (lane < slot * depth + depth)
    first = jnp.broadcast_to(lengths_ref[...].astype(F32), (8, slots))
    limit = jnp.dot(first, spread.astype(F32), preferred_element_type=F32)[:1]
    token = lax.rem(lax.broadcasted_iota(jnp.int32, (1, rows), 1), depth).astype(F32)
    turned = cotangent_ref[...].astype(F32).T
    turned_ref[...] = jnp.where(token < limit, turned, 0.0).astype(BF16)
    halves = out_ref.shape[1]
    piece = out_ref.shape[2] // pieces
    for half in range(halves):
        source = lax.rem(core_ref[0] + half, halves)
        for k in range(pieces):
            start = pl.multiple_of((k * halves + source) * piece, piece)
            block = turned_ref[pl.ds(start, piece), :]
            for copy in range(out_ref.shape[0]):
                out_ref[copy, half, pl.ds(k * piece, piece), :] = block


def partial_kernel(count, steps, here_ref, gathered_ref, own_ref, paired_ref, other_ref, *outs):
    each = gathered_ref.shape[0] // count
    piece = gathered_ref.shape[2]
    main = outs[0].shape[1]
    rest = own_ref.shape[1] - main
    block = each * piece
    turned = (((0,), (1,)), ((), ()))
    own_rest = own_ref[:, main:]
    other_rest = other_ref[:, main:]
    for k, out in zip(steps, outs):
        target = lax.rem(here_ref[0] + k, count)
        for j in range(each):
            at = target * each + j
            mine = gathered_ref[at, 0]
            theirs = paired_ref[at]
            out[pl.ds(j * piece, piece), :] = (
                jnp.dot(mine, own_ref[:, :main], preferred_element_type=F32)
                + jnp.dot(theirs, other_ref[:, :main], preferred_element_type=F32)
            ).astype(out.dtype)
            out[pl.ds(block, rest), pl.ds(j * piece, piece)] = (
                lax.dot_general(own_rest, mine, turned, preferred_element_type=F32)
                + lax.dot_general(other_rest, theirs, turned, preferred_element_type=F32)
            ).astype(out.dtype)
        out[pl.ds(block, rest), pl.ds(block, main - block)] = jnp.zeros(
            (rest, main - block), out.dtype
        )


def norm_kernel(channels, sums_ref, dy_ref, gain_ref, cnx_ref, sig_ref, cnx_out, sig_out):
    sums = sums_ref[...].T
    start = 0
    for index, (pre, out) in enumerate(((cnx_ref, cnx_out), (sig_ref, sig_out))):
        means = sums[:, index * 4 : index * 4 + 4] * (1.0 / channels[index])
        mean, grad_mean = means[:, 0:1], means[:, 2:3]
        inverse = lax.rsqrt(means[:, 1:2] - mean * mean + EPS)
        product = inverse * inverse * (means[:, 3:4] - mean * grad_mean)
        at = slice(start, start + pre.shape[1 - index])
        scaled = dy_ref[:, at].astype(F32) * gain_ref[:, at]
        height = pre[...].astype(F32)
        if index:
            height = height.T
        grad = inverse * (scaled - grad_mean - (height - mean) * product)
        out[...] = (grad.T if index else grad).astype(BF16)
        start += pre.shape[1]


def shards(
    feat_sig,
    feat_cnx,
    cotangent,
    w_sig,
    w_cnx,
    lengths,
    enc_of,
    owner_of,
    pre_sig,
    pre_cnx,
    gain_sig,
    gain_cnx,
):
    slots = lengths.shape[1]
    rows, cols = cotangent.shape
    depth = rows // slots
    enc_count = lax.axis_size("enc")
    rep_count = lax.axis_size("rep")
    nx, nz = lax.axis_size("x"), lax.axis_size("z")
    hx = lax.axis_index("x")
    core = lax.axis_index("rep")
    swap = shift(rep_count, 1)

    token = lax.broadcasted_iota(jnp.int32, (slots, depth), 1)
    chips = slots // enc_count
    piece = cols // chips // rep_count
    half = cols // rep_count
    copies = pl.pallas_call(
        functools.partial(turn_kernel, chips),
        out_shape=jax.ShapeDtypeStruct((enc_count, rep_count, half, rows), BF16),
        in_specs=[SMEM, VMEM, VMEM],
        out_specs=VMEM,
        scratch_shapes=[pltpu.VMEM((cols, rows), BF16)],
        name="turn",
    )(core.reshape(1), lengths, cotangent)
    gathered = exchange(copies, "enc")
    features = jnp.concatenate([feat_cnx, feat_sig], axis=1)
    other_features = lax.ppermute(features, "rep", swap)
    weight = jnp.concatenate([w_cnx, w_sig], axis=1)
    width = weight.shape[1]
    weight = weight.reshape(enc_count, chips, rep_count, piece, width)
    weight = jnp.stack(
        [
            lax.dynamic_index_in_dim(weight, index, 2, keepdims=False).reshape(enc_count, half, width)
            for index in (core, 1 - core)
        ],
        axis=1,
    ).reshape(enc_count * cols, width)
    gains = jnp.concatenate([gain_cnx, gain_sig])[None, :]
    gathered, other_features, weight, gains = lax.optimization_barrier(
        (gathered, other_features, weight, gains)
    )

    paired = lax.ppermute(gathered[:, 1], "rep", swap)

    block = enc_count * half // nx
    main = width // 128 * 128
    tall = block + width - main

    def multiply(steps):
        return list(
            pl.pallas_call(
                functools.partial(partial_kernel, nx, steps),
                out_shape=[
                    jax.ShapeDtypeStruct((tall, main), BF16 if k else F32) for k in steps
                ],
                in_specs=[SMEM, VMEM, VMEM, VMEM, VMEM],
                out_specs=[VMEM] * len(steps),
                compiler_params=pltpu.CompilerParams(vmem_limit_bytes=32 * 2**20),
                cost_estimate=pl.CostEstimate(
                    flops=4 * block * len(steps) * rows * width,
                    bytes_accessed=4 * block * len(steps) * width,
                    transcendentals=0,
                ),
                name="partial",
            )(hx.reshape(1), gathered, features, paired, other_features)
        )

    first = 1
    (first_part,) = multiply([first])
    first_got = lax.ppermute(first_part, "x", shift(nx, first))

    row = lax.broadcasted_iota(jnp.int32, (rows, rows), 0)
    column = lax.broadcasted_iota(jnp.int32, (rows, rows), 1)
    back = lax.dot_general(
        gathered.reshape(enc_count * cols, rows),
        weight,
        (((0,), (0,)), ((), ())),
        preferred_element_type=F32,
    ).astype(BF16)
    goal = ((enc_of[0] * depth)[:, None] + token).reshape(1, rows)
    held = pick(row == goal, back).reshape(slots, depth, width)
    held, first_part = lax.optimization_barrier((held, first_part))
    held = exchange(held, ("x", "z")).reshape(rows, width)
    place = ((owner_of[0] * depth)[:, None] + token).reshape(rows, 1)
    routed = pick(column == place, held)

    parts = multiply([k for k in range(nx) if k != first])
    parts.insert(first, first_part)
    parts = [
        first_got if k == first else lax.ppermute(part, "x", shift(nx, k)) if k else part
        for k, part in enumerate(parts)
    ]
    total = sum((part.astype(F32) for part in parts[1:]), parts[0]).astype(BF16)
    total = jnp.concatenate([total[:block], total[block:, :block].T], axis=1)
    split = feat_cnx.shape[1]

    sums = []
    for dy, gain, pre in (
        (routed[:, :split], gain_cnx, pre_cnx),
        (routed[:, split:], gain_sig, pre_sig),
    ):
        height = pre.astype(F32)
        scaled = dy.astype(F32) * gain
        sums += [
            jnp.sum(height, axis=1),
            jnp.sum(height * height, axis=1),
            jnp.sum(scaled, axis=1),
            jnp.sum(scaled * height, axis=1),
        ]
    sums, total = lax.optimization_barrier((jnp.stack(sums), total))
    total = exchange(total.reshape(nz, block // nz, width), "z")
    sums = lax.psum(sums, "enc")
    before_cnx, before_sig = pl.pallas_call(
        functools.partial(
            norm_kernel, (gain_cnx.shape[0] * enc_count, gain_sig.shape[0] * enc_count)
        ),
        out_shape=[
            jax.ShapeDtypeStruct(pre_cnx.shape, BF16),
            jax.ShapeDtypeStruct(pre_sig.shape[::-1], BF16),
        ],
        in_specs=[VMEM] * 5,
        out_specs=[VMEM] * 2,
        cost_estimate=pl.CostEstimate(flops=1, bytes_accessed=1, transcendentals=0),
        name="norm",
    )(sums, routed, gains, pre_cnx, pre_sig.T)
    scale = 1.0 / math.sqrt(rows * nx * nz * rep_count)
    grad_cnx = jnp.sum(total[:, :, :split].astype(F32), axis=0) * scale
    grad_sig = jnp.sum(total[:, :, split:].astype(F32), axis=0) * scale
    return (grad_sig, grad_cnx, before_sig.T, before_cnx)


def solution(mesh):
    enc, dp, rep = mesh.devices.shape
    along_x = 4 if dp == 64 else 2
    mesh = Mesh(
        mesh.devices.reshape(enc, along_x, dp // along_x, rep), ("enc", "x", "z", "rep")
    )
    owners = ("x", "z", "rep")
    both = P(owners, "enc")
    in_specs = (
        both,
        both,
        both,
        P(None, "enc"),
        P(None, "enc"),
        P(owners, None),
        P(owners, None),
        P(owners, None),
        both,
        both,
        P("enc"),
        P("enc"),
    )
    return jax.shard_map(
        shards, mesh=mesh, in_specs=in_specs, out_specs=(both,) * 4, check_vma=False
    )
```

```python
import functools
import math

import jax
import jax.numpy as jnp
from jax import lax
from jax.experimental import pallas as pl
from jax.experimental.pallas import tpu as pltpu
from jax.sharding import Mesh
from jax.sharding import PartitionSpec as P

EPS = 1e-06
F32 = jnp.float32
BF16 = jnp.bfloat16
VMEM = pl.BlockSpec(memory_space=pltpu.VMEM)
SMEM = pl.BlockSpec(memory_space=pltpu.SMEM)


def shift(count, step):
    return [(i, (i + step) % count) for i in range(count)]


def exchange(blocks, axis):
    return lax.all_to_all(blocks, axis, 0, 0, tiled=True)


def pick(chosen, source):
    return jnp.dot(chosen.astype(BF16), source, preferred_element_type=F32).astype(BF16)


def turn_kernel(pieces, core_ref, lengths_ref, cotangent_ref, out_ref, turned_ref):
    rows = cotangent_ref.shape[0]
    slots = lengths_ref.shape[1]
    depth = rows // slots
    lane = lax.broadcasted_iota(jnp.int32, (slots, rows), 1)
    slot = lax.broadcasted_iota(jnp.int32, (slots, rows), 0)
    spread = (lane >= slot * depth) & (lane < slot * depth + depth)
    first = jnp.broadcast_to(lengths_ref[...].astype(F32), (8, slots))
    limit = jnp.dot(first, spread.astype(F32), preferred_element_type=F32)[:1]
    token = lax.rem(lax.broadcasted_iota(jnp.int32, (1, rows), 1), depth).astype(F32)
    turned = cotangent_ref[...].astype(F32).T
    turned_ref[...] = jnp.where(token < limit, turned, 0.0).astype(BF16)
    halves = out_ref.shape[1]
    piece = out_ref.shape[2] // pieces
    for half in range(halves):
        source = lax.rem(core_ref[0] + half, halves)
        for k in range(pieces):
            start = pl.multiple_of((k * halves + source) * piece, piece)
            block = turned_ref[pl.ds(start, piece), :]
            for copy in range(out_ref.shape[0]):
                out_ref[copy, half, pl.ds(k * piece, piece), :] = block


def partial_kernel(count, steps, here_ref, gathered_ref, own_ref, paired_ref, other_ref, *outs):
    each = gathered_ref.shape[0] // count
    piece = gathered_ref.shape[2]
    main = outs[0].shape[1]
    rest = own_ref.shape[1] - main
    block = each * piece
    turned = (((0,), (1,)), ((), ()))
    own_rest = own_ref[:, main:]
    other_rest = other_ref[:, main:]
    for k, out in zip(steps, outs):
        target = lax.rem(here_ref[0] + k, count)
        for j in range(each):
            at = target * each + j
            mine = gathered_ref[at, 0]
            theirs = paired_ref[at]
            out[pl.ds(j * piece, piece), :] = (
                jnp.dot(mine, own_ref[:, :main], preferred_element_type=F32)
                + jnp.dot(theirs, other_ref[:, :main], preferred_element_type=F32)
            ).astype(out.dtype)
            out[pl.ds(block, rest), pl.ds(j * piece, piece)] = (
                lax.dot_general(own_rest, mine, turned, preferred_element_type=F32)
                + lax.dot_general(other_rest, theirs, turned, preferred_element_type=F32)
            ).astype(out.dtype)
        out[pl.ds(block, rest), pl.ds(block, main - block)] = jnp.zeros(
            (rest, main - block), out.dtype
        )


def norm_kernel(channels, sums_ref, dy_ref, gain_ref, pre_ref, cnx_out, sig_out):
    sums = sums_ref[...].T
    split = cnx_out.shape[1]
    for index, at in enumerate((slice(0, split), slice(split, pre_ref.shape[1]))):
        means = sums[:, index * 4 : index * 4 + 4] * (1.0 / channels[index])
        mean, grad_mean = means[:, 0:1], means[:, 2:3]
        inverse = lax.rsqrt(means[:, 1:2] - mean * mean + EPS)
        product = inverse * inverse * (means[:, 3:4] - mean * grad_mean)
        scaled = dy_ref[:, at].astype(F32) * gain_ref[:, at]
        height = pre_ref[:, at].astype(F32)
        grad = inverse * (scaled - grad_mean - (height - mean) * product)
        if index:
            sig_out[...] = grad.T.astype(BF16)
        else:
            cnx_out[...] = grad.astype(BF16)


def shards(
    feat_sig,
    feat_cnx,
    cotangent,
    w_sig,
    w_cnx,
    lengths,
    enc_of,
    owner_of,
    pre_sig,
    pre_cnx,
    gain_sig,
    gain_cnx,
):
    slots = lengths.shape[1]
    rows, cols = cotangent.shape
    depth = rows // slots
    enc_count = lax.axis_size("enc")
    rep_count = lax.axis_size("rep")
    nx, nz = lax.axis_size("x"), lax.axis_size("z")
    hx = lax.axis_index("x")
    core = lax.axis_index("rep")
    swap = shift(rep_count, 1)

    token = lax.broadcasted_iota(jnp.int32, (slots, depth), 1)
    chips = slots // enc_count
    piece = cols // chips // rep_count
    half = cols // rep_count
    copies = pl.pallas_call(
        functools.partial(turn_kernel, chips),
        out_shape=jax.ShapeDtypeStruct((enc_count, rep_count, half, rows), BF16),
        in_specs=[SMEM, VMEM, VMEM],
        out_specs=VMEM,
        scratch_shapes=[pltpu.VMEM((cols, rows), BF16)],
        name="turn",
    )(core.reshape(1), lengths, cotangent)
    gathered = exchange(copies, "enc")
    features = jnp.concatenate([feat_cnx, feat_sig], axis=1)
    other_features = lax.ppermute(features, "rep", swap)
    weight = jnp.concatenate([w_cnx, w_sig], axis=1)
    width = weight.shape[1]
    weight = weight.reshape(enc_count, chips, rep_count, piece, width)
    weight = jnp.stack(
        [
            lax.dynamic_index_in_dim(weight, index, 2, keepdims=False).reshape(enc_count, half, width)
            for index in (core, 1 - core)
        ],
        axis=1,
    ).reshape(enc_count * cols, width)
    gains = jnp.concatenate([gain_cnx, gain_sig])[None, :]
    gathered, other_features, weight, gains = lax.optimization_barrier(
        (gathered, other_features, weight, gains)
    )

    paired = lax.ppermute(gathered[:, 1], "rep", swap)

    block = enc_count * half // nx
    main = width // 128 * 128
    tall = block + width - main

    def multiply(steps):
        return list(
            pl.pallas_call(
                functools.partial(partial_kernel, nx, steps),
                out_shape=[
                    jax.ShapeDtypeStruct((tall, main), BF16 if k else F32) for k in steps
                ],
                in_specs=[SMEM, VMEM, VMEM, VMEM, VMEM],
                out_specs=[VMEM] * len(steps),
                compiler_params=pltpu.CompilerParams(vmem_limit_bytes=32 * 2**20),
                cost_estimate=pl.CostEstimate(
                    flops=4 * block * len(steps) * rows * width,
                    bytes_accessed=4 * block * len(steps) * width,
                    transcendentals=0,
                ),
                name="partial",
            )(hx.reshape(1), gathered, features, paired, other_features)
        )

    far = nx // 2
    (far_part,) = multiply([far])
    far_got = lax.ppermute(far_part, "x", shift(nx, far))

    row = lax.broadcasted_iota(jnp.int32, (rows, rows), 0)
    column = lax.broadcasted_iota(jnp.int32, (rows, rows), 1)
    back = lax.dot_general(
        gathered.reshape(enc_count * cols, rows),
        weight,
        (((0,), (0,)), ((), ())),
        preferred_element_type=F32,
    ).astype(BF16)
    goal = ((enc_of[0] * depth)[:, None] + token).reshape(1, rows)
    held = pick(row == goal, back).reshape(slots, depth, width)
    held, far_part = lax.optimization_barrier((held, far_part))
    held = exchange(held, ("x", "z")).reshape(rows, width)

    parts = multiply([k for k in range(nx) if k != far])
    parts.insert(far, far_part)
    parts = [
        far_got if k == far else lax.ppermute(part, "x", shift(nx, k)) if k else part
        for k, part in enumerate(parts)
    ]
    total = sum((part.astype(F32) for part in parts[1:]), parts[0]).astype(BF16)
    total = jnp.concatenate([total[:block], total[block:, :block].T], axis=1)
    split = feat_cnx.shape[1]

    heights = jnp.concatenate([pre_cnx, pre_sig], axis=1)
    place = ((owner_of[0] * depth)[:, None] + token).reshape(rows, 1)
    held, total, heights, place = lax.optimization_barrier((held, total, heights, place))
    total = exchange(total.reshape(nz, block // nz, width), "z")
    routed = pick(column == place, held)
    sums = []
    for dy, gain, pre in (
        (routed[:, :split], gain_cnx, heights[:, :split]),
        (routed[:, split:], gain_sig, heights[:, split:]),
    ):
        height = pre.astype(F32)
        scaled = dy.astype(F32) * gain
        sums += [
            jnp.sum(height, axis=1),
            jnp.sum(height * height, axis=1),
            jnp.sum(scaled, axis=1),
            jnp.sum(scaled * height, axis=1),
        ]
    sums = lax.psum(jnp.stack(sums), "enc")
    before_cnx, before_sig = pl.pallas_call(
        functools.partial(
            norm_kernel, (gain_cnx.shape[0] * enc_count, gain_sig.shape[0] * enc_count)
        ),
        out_shape=[
            jax.ShapeDtypeStruct(pre_cnx.shape, BF16),
            jax.ShapeDtypeStruct(pre_sig.shape[::-1], BF16),
        ],
        in_specs=[VMEM] * 4,
        out_specs=[VMEM] * 2,
        cost_estimate=pl.CostEstimate(flops=1, bytes_accessed=1, transcendentals=0),
        name="norm",
    )(sums, routed, gains, heights)
    scale = 1.0 / math.sqrt(rows * nx * nz * rep_count)
    grad_cnx = jnp.sum(total[:, :, :split].astype(F32), axis=0) * scale
    grad_sig = jnp.sum(total[:, :, split:].astype(F32), axis=0) * scale
    return (grad_sig, grad_cnx, before_sig.T, before_cnx)


def solution(mesh):
    enc, dp, rep = mesh.devices.shape
    along_x = 4 if dp == 64 else 2
    mesh = Mesh(
        mesh.devices.reshape(enc, along_x, dp // along_x, rep), ("enc", "x", "z", "rep")
    )
    owners = ("x", "z", "rep")
    both = P(owners, "enc")
    in_specs = (
        both,
        both,
        both,
        P(None, "enc"),
        P(None, "enc"),
        P(owners, None),
        P(owners, None),
        P(owners, None),
        both,
        both,
        P("enc"),
        P("enc"),
    )
    return jax.shard_map(
        shards, mesh=mesh, in_specs=in_specs, out_specs=(both,) * 4, check_vma=False
    )
```
